512 devices in a mesh: pipe: 4 (over x), rep: 4 (over y_lo, core), ep: 32 (over z, y_hi).
Axes of the slice: x: 4, y: 8 (y_hi: 4, y_lo: 2; y = y_hi * 2 + y_lo), z: 8, core: 2. Of those that a mesh axis runs over, the one named last changes fastest.
Arguments:
- a_sent: bfloat16 [4, 4096, 3584], P('pipe', 'ep', 'rep'), may hold values from -6 to 6
- b_input: bfloat16 [4, 4096, 3584], P('pipe', 'ep', 'rep'), may hold values from -6 to 6
- b_grad: bfloat16 [4, 4096, 3584], P('pipe', 'ep', 'rep'), may hold values from -6 to 6
- routes_a: int32 [4, 4096, 8], P('pipe', 'ep'), may hold values from 0 to 255, all different within a row; in each aligned block of 128 rows (0 to 127, 128 to 255, ..., all dimensions but the last counted through in order) at most 8 rows name the same one
- routes_b: int32 [4, 4096, 8], P('pipe', 'ep'), may hold values from 0 to 255, all different within a row; in each aligned block of 128 rows (0 to 127, 128 to 255, ..., all dimensions but the last counted through in order) at most 8 rows name the same one
- gates_a: bfloat16 [4, 4096, 8], P('pipe', 'ep'), may hold values from 0.049804688 to 0.59765625
- gates_b: bfloat16 [4, 4096, 8], P('pipe', 'ep'), may hold values from 0.049804688 to 0.59765625
- w_in: bfloat16 [4, 32, 3584, 4, 256], P('pipe', 'ep', None, 'rep'), may hold values from -0.09375 to 0.09375
- w_down: bfloat16 [4, 32, 3584, 4, 128], P('pipe', 'ep', None, 'rep'), may hold values from -0.1875 to 0.1875
Outputs:
- y_a: bfloat16 [4, 4096, 3584], P('pipe', 'ep', 'rep')
- dx_b: bfloat16 [4, 4096, 3584], P('pipe', 'ep', 'rep')
- dgate_b: bfloat16 [4, 4096, 8], P('pipe', 'ep')
The draws below stay inside these ranges and needn't reach their ends.
Inputs may be any that keep to these rules, and one draw needn't show every extreme that they name: `routes_a`: each row names 8 different numbers; in the rows of one device no number is named by more than 8 rows. `routes_b`: each row names 8 different numbers; in the rows of one device no number is named by more than 8 rows.
All inputs are finite; a program needn't handle non-finite values.
Results may differ from the reference program's by a relative error of at most 0.015.
Values may be sent and summed in bfloat16 or wider, within the bound.
No kernel may reach another device: no remote copies, remote signals or barrier semaphores. Data moves between devices by JAX's collectives and lax.ppermute only.
A program may use at most 64 MiB of HBM per device.

```python
import math
import jax
import jax.numpy as jnp
import numpy as np
from jax import lax

D = 3584
NE = 256
TOPK = 8
HID = 1024
TOK = 128
CAP = 8
SECTIONS = 4
EXPERTS = 16
HSH = 128
ROWS = 4096
N_REP = 4
N_EP = 32


def steps_of(stream_key, dims, shards, low, high):
    def one(dim, shards_of):
        heights = jax.random.uniform(jax.random.fold_in(jax.random.fold_in(stream_key, 6), dim), (shards_of,), jnp.float32, low / len(shards), high / len(shards))
        return jnp.repeat(jnp.exp(heights), dims[dim] // shards_of).reshape((-1,) + (1,) * (len(dims) - dim - 1))

    loudness = one(*shards[0])
    for cut in shards[1:]:
        loudness = loudness * one(*cut)
    return loudness


def routed_block(key, own, number, rows, amount, top, most, lean):
    sequence = jax.random.permutation(key, amount)
    heavy_load, usual = portions_of(amount, rows * top, most, lean, True), portions_of(amount, rows * top, most, lean, False)
    places = jnp.arange(amount)

    def named(tallies, rotation):
        used = int((tallies > 0).sum())
        fixed = max(1, used // 4)
        shifted = fixed + (places - fixed + rotation * (used - fixed)) % max(1, amount - fixed)
        return jnp.zeros((amount,), jnp.int32).at[sequence[jnp.where(places < fixed, places, shifted)]].set(jnp.asarray(tallies, jnp.int32))

    tallies = jnp.where(number % 4 == 0, named(heavy_load, number // 4), named(usual, number - number // 4 - 1))
    mixed = jax.random.permutation(jax.random.fold_in(own, 3), amount)
    source_of, taker = mixed[0:amount // 2 * 2:2], mixed[1:amount // 2 * 2:2]
    slack = jnp.minimum(tallies[source_of] - 1, most - tallies[taker]) // 2
    slack = jnp.where((source_of == sequence[0]) | (taker == sequence[0]) | (tallies[taker] == 0), 0, jnp.maximum(slack, 0))
    shifted = jax.random.randint(jax.random.fold_in(own, 4), (amount // 2,), 0, 1 << 20) % (slack + 1)
    tallies = tallies.at[source_of].add(-shifted).at[taker].add(shifted)
    members = jnp.searchsorted(jnp.cumsum(tallies), jnp.arange(rows * top), side="right").astype(jnp.int32)
    listing = members.reshape(top, rows).T
    listing = listing[jax.random.permutation(jax.random.fold_in(own, 1), rows)]
    rotation = jax.random.randint(jax.random.fold_in(own, 2), (rows, 1), 0, top)
    return jnp.take_along_axis(listing, (jnp.arange(top)[None, :] + rotation) % top, axis=1)


def portions_of(amount, total, reach, slope, full):
    portions = [(1 << 20) // math.isqrt(standing ** slope) + 1 for standing in range(1, amount + 1)]
    largest = reach if full else min(reach, max(-(-total // amount), total * portions[0] // sum(portions)))
    least = 1 if total - largest >= amount - 1 else 0
    holding, spare = [largest] + [least] * (amount - 1), total - largest - least * (amount - 1)
    while spare > 0:
        free = [i for i in range(1, amount) if holding[i] < largest] or [i for i in range(1, amount) if holding[i] < reach]
        pool, left = sum([portions[i] for i in free]), spare
        for i in free:
            extra = min(reach - holding[i], max(1, left * portions[i] // pool), spare)
            holding[i] = holding[i] + extra
            spare = spare - extra
    return np.array(holding)


def normal_values(key, shape, deviation, bound, cuts=(), held_as=jnp.bfloat16):
    array = jax.random.normal(key, shape, jnp.float32) * deviation
    if len(cuts) > 0:
        array = steps_of(key, shape, cuts, -0.22, 0.18) * array
    return jnp.clip(array, min=-bound, max=bound).astype(held_as)


def setup_inputs(seed: int = 0) -> dict:
    keys = jax.random.split(jax.random.key(seed), 10)
    a_sent = normal_values(keys[0], (SECTIONS, ROWS, D), 1.0, 6.0, ((0, 4), (1, 32), (2, 4)))
    b_input = normal_values(keys[1], (SECTIONS, ROWS, D), 1.0, 6.0, ((0, 4), (1, 32), (2, 4)))
    b_grad = normal_values(keys[2], (SECTIONS, ROWS, D), 1.0, 6.0, ((0, 4), (1, 32), (2, 4)))
    routes_a_keys = jax.random.split(jax.random.fold_in(keys[3], 1), SECTIONS * ROWS // TOK)
    routes_a_turns = jax.random.permutation(jax.random.fold_in(keys[3], 3), SECTIONS * ROWS // TOK)
    routes_a = jax.vmap(lambda own, number: routed_block(jax.random.fold_in(keys[3], 2), own, number, TOK, NE, TOPK, CAP, 2))(routes_a_keys, routes_a_turns).reshape((SECTIONS, ROWS, TOPK))
    routes_b_keys = jax.random.split(jax.random.fold_in(keys[4], 1), SECTIONS * ROWS // TOK)
    routes_b_turns = jax.random.permutation(jax.random.fold_in(keys[4], 3), SECTIONS * ROWS // TOK)
    routes_b = jax.vmap(lambda own, number: routed_block(jax.random.fold_in(keys[4], 2), own, number, TOK, NE, TOPK, CAP, 2))(routes_b_keys, routes_b_turns).reshape((SECTIONS, ROWS, TOPK))
    gates_a = jnp.clip(0.049804688 + 0.54785156 * jax.random.uniform(keys[5], (SECTIONS, ROWS, TOPK), jnp.float32) ** steps_of(keys[5], (SECTIONS, ROWS, TOPK), ((0, 4), (1, 32)), -0.2, 0.2), 0.049804688, 0.59765625).astype(jnp.bfloat16)
    gates_b = jnp.clip(0.049804688 + 0.54785156 * jax.random.uniform(keys[6], (SECTIONS, ROWS, TOPK), jnp.float32) ** steps_of(keys[6], (SECTIONS, ROWS, TOPK), ((0, 4), (1, 32)), -0.2, 0.2), 0.049804688, 0.59765625).astype(jnp.bfloat16)
    w_in = normal_values(keys[7], (SECTIONS, 2 * EXPERTS, D, N_REP, 2 * HSH), D ** -0.5, 0.09375, ((0, 4), (1, 32), (3, 4)))
    w_down = normal_values(keys[8], (SECTIONS, 2 * EXPERTS, D, N_REP, HSH), HID ** -0.5, 0.1875, ((0, 4), (1, 32), (3, 4)))
    return dict(a_sent=a_sent, b_input=b_input, b_grad=b_grad, routes_a=routes_a, routes_b=routes_b, gates_a=gates_a, gates_b=gates_b, w_in=w_in, w_down=w_down)


HIGH = lax.Precision.HIGHEST


def tables(routes, gates, experts_total, depth):
    matches = (routes[..., None] == jnp.arange(experts_total, dtype=jnp.int32)).astype(jnp.int32)
    hit_count = jnp.sum(matches, axis=2)
    weight = jnp.sum(gates.astype(jnp.float32)[..., None] * matches.astype(jnp.float32), axis=2)
    before = jnp.cumsum(hit_count, axis=1) - hit_count
    select = hit_count[..., None] * (before[..., None] == jnp.arange(depth, dtype=jnp.int32)).astype(jnp.int32)
    return matches, select.astype(jnp.float32), weight


def pick_rows(select, values):
    picked = jnp.einsum('btec,btd->becd', select, values.astype(jnp.float32), precision=HIGH)
    return picked.astype(jnp.bfloat16)


def to_experts(values):
    reordered = jnp.moveaxis(values, 1, 0)
    return reordered.reshape((reordered.shape[0], reordered.shape[1] * reordered.shape[2]) + reordered.shape[3:])


def from_experts(values):
    trailing = values.shape[3:]
    reordered = values.reshape((EXPERTS, 2, N_EP, CAP) + trailing)
    return jnp.moveaxis(reordered, 2, 0)


def widen(values):
    return lax.optimization_barrier(values).astype(jnp.float32)


def block_forward(rows, w_block, down_block):
    units = down_block.shape[1]
    gate_up = jnp.dot(rows, w_block, preferred_element_type=jnp.float32)
    hidden = (jax.nn.silu(gate_up[:, :units]) * gate_up[:, units:]).astype(jnp.bfloat16)
    output = lax.dot_general(hidden, down_block, (((1,), (1,)), ((), ())), preferred_element_type=jnp.float32)
    return gate_up, output


def block_backward(gate_up, d_out, w_block, down_block):
    units = down_block.shape[1]
    gate_part, up_part = gate_up[:, :units], gate_up[:, units:]
    d_hidden = jnp.dot(d_out, down_block, preferred_element_type=jnp.float32)
    squash = jax.nn.sigmoid(gate_part)
    d_gate = (d_hidden * up_part * squash * (1.0 + gate_part * (1.0 - squash))).astype(jnp.bfloat16)
    d_up = (d_hidden * gate_part * squash).astype(jnp.bfloat16)
    d_gate_up = jnp.concatenate([d_gate, d_up], axis=1)
    d_rows = lax.dot_general(d_gate_up, w_block, (((1,), (1,)), ((), ())), preferred_element_type=jnp.float32)
    return d_rows.astype(jnp.bfloat16)


def expert_all(packed):
    rows_a, rows_b, grad_rows, slot_gate, w_expert, down_expert = packed
    grads_wide = grad_rows.astype(jnp.float32)
    d_out = (slot_gate.astype(jnp.float32)[:, None] * grads_wide).astype(jnp.bfloat16)
    outs_a, outs_dx, outs_dg = [], [], []
    for half_index in range(2):
        sum_a = jnp.zeros(rows_a.shape, jnp.float32)
        sum_dx = jnp.zeros(rows_b.shape, jnp.float32)
        sum_dg = jnp.zeros((rows_b.shape[0],), jnp.float32)
        for block_index in range(N_REP):
            w_block = w_expert[half_index, :, block_index]
            down_block = down_expert[half_index, :, block_index]
            output_a = block_forward(rows_a, w_block, down_block)[1]
            sum_a = sum_a + widen(output_a.astype(jnp.bfloat16))
            gate_up_b, output_b = block_forward(rows_b, w_block, down_block)
            sum_dg = sum_dg + jnp.sum(output_b * grads_wide, axis=1)
            sum_dx = sum_dx + widen(block_backward(gate_up_b, d_out, w_block, down_block))
        outs_a.append(sum_a.astype(jnp.bfloat16))
        outs_dx.append(sum_dx.astype(jnp.bfloat16))
        outs_dg.append(sum_dg.astype(jnp.bfloat16))
    return jnp.stack(outs_a), jnp.stack(outs_dx), jnp.stack(outs_dg)


def reference(a_sent, b_input, b_grad, routes_a, routes_b, gates_a, gates_b, w_in, w_down):
    outs_y, outs_dx, outs_dg = [], [], []
    for section in range(SECTIONS):
        input_a = a_sent[(section - 1) % SECTIONS].reshape(N_EP, TOK, D)
        match_a, select_a, weight_a = tables(routes_a[section].reshape(N_EP, TOK, TOPK), gates_a[section].reshape(N_EP, TOK, TOPK), EXPERTS, CAP)
        match_b, select_b, weight_b = tables(routes_b[section].reshape(N_EP, TOK, TOPK), gates_b[section].reshape(N_EP, TOK, TOPK), EXPERTS, CAP)
        rows_a = to_experts(pick_rows(select_a, input_a))
        rows_b = to_experts(pick_rows(select_b, b_input[section].reshape(N_EP, TOK, D)))
        grad_rows = to_experts(pick_rows(select_b, b_grad[section].reshape(N_EP, TOK, D)))
        slot_gate = jnp.einsum('btec,bte->bec', select_b, weight_b, precision=HIGH).astype(jnp.bfloat16)
        slot_gate = to_experts(slot_gate)
        w_section = w_in[section].reshape(EXPERTS, 2, D, N_REP, w_in.shape[4])
        down_section = w_down[section].reshape(EXPERTS, 2, D, N_REP, w_down.shape[4])
        half_a, half_dx, half_dg = lax.map(expert_all, (rows_a, rows_b, grad_rows, slot_gate, w_section, down_section))
        combined = jnp.einsum('btec,behcd->btd', select_a * weight_a[..., None], widen(from_experts(half_a)), precision=HIGH)
        outs_y.append(combined.astype(jnp.bfloat16).reshape(ROWS, D))
        grad_in = jnp.einsum('btec,behcd->btd', select_b, widen(from_experts(half_dx)), precision=HIGH)
        outs_dx.append(grad_in.astype(jnp.bfloat16).reshape(ROWS, D))
        per_expert = jnp.einsum('btec,behc->bte', select_b, widen(from_experts(half_dg)), precision=HIGH)
        dgate = jnp.sum(match_b.astype(jnp.float32) * per_expert[:, :, None, :], axis=3)
        outs_dg.append(dgate.astype(jnp.bfloat16).reshape(ROWS, TOPK))
    return jnp.stack(outs_y), jnp.stack(outs_dx), jnp.stack(outs_dg)
```

```python
import jax
import jax.numpy as jnp
from jax import lax
from jax.sharding import PartitionSpec as P

CAP = 8
F32 = jnp.float32
BF16 = jnp.bfloat16


def passed_along(value, axis, by):
    size = lax.axis_size(axis)
    return lax.ppermute(value, axis, [(i, (i + by) % size) for i in range(size)])


def core_swap(value):
    return lax.ppermute(value, "rep", [(i, i ^ 1) for i in range(4)])


def chip_swap(value):
    return lax.ppermute(value, "rep", [(i, i ^ 2) for i in range(4)])


def over_ep(value):
    return lax.all_to_all(value, "ep", split_axis=0, concat_axis=0, tiled=True)


def tables(routes, gates, experts):
    match = (routes[:, :, None] == jnp.arange(experts, dtype=jnp.int32)).astype(F32)
    hits = jnp.sum(match, axis=1)
    weight = jnp.sum(gates.astype(F32)[:, :, None] * match, axis=1)
    rows = routes.shape[0]
    lower = jnp.tril(jnp.ones((rows, rows), BF16), -1)
    before = jnp.dot(lower, hits.astype(BF16), preferred_element_type=F32)
    select = hits[:, :, None] * (before[:, :, None] == jnp.arange(CAP, dtype=F32)).astype(F32)
    return match, select, weight


def mm(x, w):
    return jnp.dot(x, w, preferred_element_type=F32)


def mt(x, w):
    return lax.dot_general(x, w, (((1,), (1,)), ((), ())), preferred_element_type=F32)


def twice(select):
    t, e, c = select.shape
    return jnp.broadcast_to(select[:, :, None, :], (t, e, 2, c)).reshape(t, e * 2 * c)


def pick(select, values):
    t, e, c = select.shape
    n = len(values)
    eye = jnp.eye(n, dtype=F32)
    full = select[None, :, :, None, None, :] * eye[:, None, None, None, :, None]
    full = jnp.broadcast_to(full, (n, t, e, 2, n, c)).reshape(n * t, e * 2 * n * c).astype(BF16)
    stacked = values[0] if n == 1 else jnp.concatenate(values, axis=0)
    out = lax.dot_general(full, stacked, (((0,), (0,)), ((), ())), preferred_element_type=F32)
    return out.astype(BF16).reshape(e * 2, n * c, -1)


def on_device(a_sent, b_input, b_grad, routes_a, routes_b, gates_a, gates_b, w_in, w_down):
    experts = lax.axis_size("ep") // 2
    sources = 2 * experts
    rep = lax.axis_index("rep")
    dl = a_sent.shape[2]
    input_a = passed_along(a_sent, "pipe", 1)[0]

    match_b, select_b, weight_b = tables(routes_b[0], gates_b[0], experts)
    match_a, select_a, weight_a = tables(routes_a[0], gates_a[0], experts)

    got_bg = over_ep(pick(select_b, [b_input[0], b_grad[0]]))

    wi, wd = w_in[0, 0, :, 0, :], w_down[0, 0, :, 0, :]

    def part(w, index):
        return lax.dynamic_slice_in_dim(w, index * dl, dl, axis=0)

    wi_own, wi_oth = part(wi, rep), part(wi, rep ^ 1)
    wd_own, wd_oth = part(wd, rep), part(wd, rep ^ 1)
    wi_peer = chip_swap(jnp.concatenate([part(wi, rep ^ 2), part(wi, rep ^ 3)], axis=0))
    wd_peer = chip_swap(jnp.concatenate([part(wd, rep ^ 2), part(wd, rep ^ 3)], axis=0))
    wi_pown, wi_poth = wi_peer[:dl], wi_peer[dl:]
    wd_pown, wd_poth = wd_peer[:dl], wd_peer[dl:]

    got_a = over_ep(pick(select_a, [input_a]))

    oth_bg = core_swap(got_bg)
    xo, go = got_bg[:, :CAP].reshape(-1, dl), got_bg[:, CAP:].reshape(-1, dl)
    xt, gt = oth_bg[:, :CAP].reshape(-1, dl), oth_bg[:, CAP:].reshape(-1, dl)
    units = wd.shape[1]
    to_peer = jnp.concatenate(
        [mm(xo, wi_pown) + mm(xt, wi_poth), mm(go, wd_pown) + mm(gt, wd_poth)], axis=1
    ).astype(BF16)
    from_peer = chip_swap(to_peer).astype(F32)
    gu = mm(xo, wi_own) + mm(xt, wi_oth) + from_peer[:, : 2 * units]
    dh = mm(go, wd_own) + mm(gt, wd_oth) + from_peer[:, 2 * units :]
    g, u = gu[:, :units], gu[:, units:]
    sq = jax.nn.sigmoid(g)
    hid = (g * sq * u).astype(BF16)
    dg_part = jnp.sum(hid.astype(F32) * dh, axis=1).astype(BF16)
    d_gate = (dh * u * sq * (1.0 + g * (1.0 - sq))).astype(BF16)
    d_up = (dh * g * sq).astype(BF16)
    dgu = jnp.concatenate([d_gate, d_up], axis=1)
    pad = jnp.broadcast_to(dg_part[:, None], (dg_part.shape[0], 128))
    peer_dgu = chip_swap(jnp.concatenate([dgu, pad], axis=1))
    dg_chip = (pad.astype(F32) + peer_dgu[:, 2 * units :].astype(F32)).astype(BF16)
    dgp = peer_dgu[:, : 2 * units]
    dx_oth = (mt(dgu, wi_oth) + mt(dgp, wi_poth)).astype(BF16)
    dx_got = core_swap(jnp.concatenate([dx_oth, dg_chip], axis=1))
    dx_own = mt(dgu, wi_own) + mt(dgp, wi_pown) + dx_got[:, :dl].astype(F32)
    dg_all = dg_chip.astype(F32) + dx_got[:, dl:].astype(F32)
    back_b = over_ep(
        jnp.concatenate([dx_own, dg_all], axis=1).astype(BF16).reshape(sources, CAP, -1)
    )

    oth_a = core_swap(got_a)
    ao, at = got_a.reshape(-1, dl), oth_a.reshape(-1, dl)
    ga_peer = chip_swap((mm(ao, wi_pown) + mm(at, wi_poth)).astype(BF16))
    gu_a = mm(ao, wi_own) + mm(at, wi_oth) + ga_peer.astype(F32)
    hid_a = (jax.nn.silu(gu_a[:, :units]) * gu_a[:, units:]).astype(BF16)
    hid_p = chip_swap(hid_a)
    o_oth = core_swap((mt(hid_a, wd_oth) + mt(hid_p, wd_poth)).astype(BF16))
    o_own = mt(hid_a, wd_own) + mt(hid_p, wd_pown) + o_oth.astype(F32)
    back_a = over_ep(o_own.astype(BF16).reshape(sources, CAP, dl))

    dx = mm(twice(select_b * weight_b[:, :, None]).astype(BF16), back_b[:, :, :dl].reshape(-1, dl))
    dgs = back_b[:, :, dl].astype(F32).reshape(experts, 2, CAP)
    dgs = dgs[:, 0] + dgs[:, 1]
    per_expert = jnp.sum(select_b * dgs[None], axis=2)
    dgate = jnp.sum(match_b * per_expert[:, None, :], axis=2)
    y = mm(twice(select_a * weight_a[:, :, None]).astype(BF16), back_a.reshape(-1, dl))
    return y.astype(BF16)[None], dx.astype(BF16)[None], dgate.astype(BF16)[None]


def solution(mesh):
    rows = P("pipe", "ep", "rep")
    small = P("pipe", "ep", None)
    weights = P("pipe", "ep", None, "rep", None)
    return jax.shard_map(
        on_device,
        mesh=mesh,
        in_specs=(rows, rows, rows, small, small, small, small, weights, weights),
        out_specs=(rows, rows, small),
        check_vma=False,
    )
```

```python
import jax
import jax.numpy as jnp
from jax import lax
from jax.experimental import pallas as pl
from jax.experimental.pallas import tpu as pltpu
from jax.sharding import Mesh
from jax.sharding import PartitionSpec as P

CAP = 8
NY = 4
F32 = jnp.float32
BF16 = jnp.bfloat16
VMEM = pl.BlockSpec(memory_space=pltpu.VMEM)


def call(kernel, outs, args, flops):
    moved = sum(x.size * x.dtype.itemsize for x in (*args, *outs))
    return pl.pallas_call(
        kernel,
        out_shape=outs,
        in_specs=[VMEM] * len(args),
        out_specs=[VMEM] * len(outs),
        compiler_params=pltpu.CompilerParams(vmem_limit_bytes=24 << 20),
        cost_estimate=pl.CostEstimate(flops=flops, bytes_accessed=moved, transcendentals=0),
    )(*args)


def like(shape, dtype=BF16):
    return jax.ShapeDtypeStruct(shape, dtype)


def ring(axis, by):
    size = lax.axis_size(axis)
    return [(i, (i + by) % size) for i in range(size)]


def core_swap(value):
    return lax.ppermute(value, "rep", [(i, i ^ 1) for i in range(4)])


def chip_swap(value):
    return lax.ppermute(value, "rep", [(i, i ^ 2) for i in range(4)])


def mm(x, w):
    return jnp.dot(x, w, preferred_element_type=F32)


def mt(x, w):
    return lax.dot_general(x, w, (((1,), (1,)), ((), ())), preferred_element_type=F32)


def lanes_of(width):
    return lax.broadcasted_iota(jnp.int32, (1, width), 1)


def slot_table(routes, gates, width, per_expert):
    rows = routes.shape[0]
    lane = lanes_of(width)
    expert = lane // per_expert
    hit = jnp.zeros((rows, width), F32)
    weight = jnp.zeros((rows, width), F32)
    for k in range(routes.shape[1]):
        named = routes[:, k : k + 1] == expert
        hit = jnp.where(named, 1.0, hit)
        weight = jnp.where(named, gates[:, k : k + 1], weight)
    row = lax.broadcasted_iota(jnp.int32, (rows, rows), 0)
    col = lax.broadcasted_iota(jnp.int32, (rows, rows), 1)
    lower = jnp.where(col < row, 1.0, 0.0).astype(BF16)
    before = mm(lower, hit.astype(BF16))
    select = jnp.where(before == (lane % CAP).astype(F32), hit, 0.0)
    return select, weight * select


def tables_kernel(ra, rb, ga, gb, sel_a, sel_b, sel2_b, wt_a, wt_b):
    slots = sel_a.shape[1]
    for r, g, sel, sel2, wt in ((ra, ga, sel_a, None, wt_a), (rb, gb, sel_b, sel2_b, wt_b)):
        routes, gates = r[...], g[...].astype(F32)
        sel[...] = slot_table(routes, gates, slots, CAP)[0].astype(BF16)
        two, weight = slot_table(routes, gates, 2 * slots, 2 * CAP)
        wt[...] = weight.astype(BF16)
        if sel2 is not None:
            sel2[...] = two.astype(BF16)


def pick_kernel(sel_a, sel_b, a, b, g, out):
    def picked(sel, x):
        return lax.dot_general(
            sel[...], x[...], (((0,), (0,)), ((), ())), preferred_element_type=F32
        )

    parts = [picked(sel_a, a), picked(sel_b, b), picked(sel_b, g)]
    for z in range(out.shape[0]):
        rows = [
            p[(2 * z + m) * CAP : (2 * z + m + 1) * CAP] for m in range(2) for p in parts
        ]
        out[z] = jnp.concatenate(rows, axis=0).astype(BF16)


def features_kernel(index, wi, wd, out):
    units = wd.shape[1]
    out[:, : 2 * units] = wi[...]
    out[:, 2 * units :] = wd[...]


def spread_kernel(z_rows, out):
    nz = z_rows.shape[0]
    wide = [z_rows[z].astype(F32) for z in range(nz)]
    for m in range(2):
        rows = [
            wide[z][(3 * m + q) * CAP : (3 * m + q + 1) * CAP] for q in range(3) for z in range(nz)
        ]
        both = jnp.concatenate(rows, axis=0).astype(BF16)
        out[2 * m] = both
        out[2 * m + 1] = both


def first_a_kernel(own, oth, w, out):
    dl, units2 = own.shape[2], out.shape[2]
    n = out.shape[1]
    for s in range(NY):
        x = mm(own[s, :n], w[:dl, :units2]) + mm(oth[s, :n], w[dl:, :units2])
        out[s] = x.astype(out.dtype)


def first_b_kernel(own, oth, w, out):
    dl = own.shape[2]
    n, units = out.shape[1], out.shape[2] // 3
    for s in range(NY):
        x, g = slice(n, 2 * n), slice(2 * n, 3 * n)
        gu = mm(own[s, x], w[:dl, : 2 * units]) + mm(oth[s, x], w[dl:, : 2 * units])
        dh = mm(own[s, g], w[:dl, 2 * units :]) + mm(oth[s, g], w[dl:, 2 * units :])
        out[s, :, : 2 * units] = gu.astype(out.dtype)
        out[s, :, 2 * units :] = dh.astype(out.dtype)


def by_source(value):
    nz = value.shape[0] // (NY * CAP)
    rows = [
        value[(s * nz + z) * CAP : (s * nz + z + 1) * CAP] for z in range(nz) for s in range(NY)
    ]
    return jnp.concatenate(rows, axis=0)


def middle_a_kernel(self_ref, peer_ref, out):
    units = out.shape[1]
    v = self_ref[...] + peer_ref[...].astype(F32)
    g, u = v[:, :units], v[:, units:]
    out[...] = by_source(g * jax.nn.sigmoid(g) * u).astype(BF16)


def middle_b_kernel(self_ref, peer_ref, out):
    units = out.shape[1] // 3
    v = self_ref[...] + peer_ref[...].astype(F32)
    g, u, dh = v[:, :units], v[:, units : 2 * units], v[:, 2 * units :]
    sq = jax.nn.sigmoid(g)
    hid = (g * sq * u).astype(BF16).astype(F32)
    dgate = jnp.broadcast_to(jnp.sum(hid * dh, axis=1, keepdims=True), g.shape)
    d_gate = dh * u * sq * (1.0 + g * (1.0 - sq))
    d_up = dh * g * sq
    out[...] = by_source(jnp.concatenate([d_gate, d_up, dgate], axis=1)).astype(BF16)


def last_a_kernel(mine, peer, w_self, w_peer, out):
    units = mine.shape[1]
    o = mt(mine[...], w_self[:, 2 * units :]) + mt(peer[...], w_peer[:, 2 * units :])
    out[...] = o.astype(out.dtype)


def last_b_kernel(mine, peer, w_self, w_peer, out):
    dl = w_self.shape[0]
    units = mine.shape[1] // 3
    m, p = mine[...], peer[...]
    dx = mt(m[:, : 2 * units], w_self[:, : 2 * units]) + mt(
        p[:, : 2 * units], w_peer[:, : 2 * units]
    )
    out[:, :dl] = dx.astype(out.dtype)
    dg = (m[:, 2 * units :].astype(F32) + p[:, 2 * units :].astype(F32)).astype(BF16)
    out[:, dl:] = dg.astype(out.dtype)


def add_kernel(kept_a, core_a, kept_b, core_b, out):
    dl = kept_a.shape[1]
    out[:, :dl] = (kept_a[...] + core_a[...].astype(F32)).astype(BF16)
    out[:, dl:] = (kept_b[...] + core_b[...].astype(F32)).astype(BF16)


def combine_kernel(back, wt_a, wt_b, sel2_b, routes, y, dx, dgate):
    dl = y.shape[1]
    y[...] = mm(wt_a[...], back[:, :dl]).astype(BF16)
    dx[...] = mm(wt_b[...], back[:, dl : 2 * dl]).astype(BF16)
    dg = back[:, 2 * dl :]
    expert = lanes_of(sel2_b.shape[1]) // (2 * CAP)
    sel = sel2_b[...].astype(F32)
    topk = dgate.shape[1]
    out = jnp.zeros((sel.shape[0], dg.shape[1]), F32)
    lane = lanes_of(dg.shape[1])
    for k in range(topk):
        chosen = jnp.where(routes[:, k : k + 1] == expert, sel, 0.0).astype(BF16)
        out = jnp.where(lane == k, mm(chosen, dg), out)
    dgate[...] = out[:, :topk].astype(BF16)


def on_device(a_sent, b_input, b_grad, routes_a, routes_b, gates_a, gates_b, w_in, w_down):
    nz = lax.axis_size("z")
    sources, experts = nz * NY, nz * 2
    slots = experts * CAP
    rep = lax.axis_index("rep")
    tok, dl = a_sent.shape[1:]
    wi, wd = w_in[0, 0, :, 0, :], w_down[0, 0, :, 0, :]
    units = wd.shape[1]
    n = nz * CAP

    input_a = lax.ppermute(a_sent, "pipe", ring("pipe", 1))

    def features(*index):
        parts = len(index)
        return pl.pallas_call(
            features_kernel,
            out_shape=like((parts * dl, 3 * units)),
            grid_spec=pltpu.PrefetchScalarGridSpec(
                num_scalar_prefetch=1,
                grid=(parts,),
                in_specs=[
                    pl.BlockSpec((dl, 2 * units), lambda i, index: (index[i], 0)),
                    pl.BlockSpec((dl, units), lambda i, index: (index[i], 0)),
                ],
                out_specs=pl.BlockSpec((dl, 3 * units), lambda i, index: (i, 0)),
            ),
            compiler_params=pltpu.CompilerParams(vmem_limit_bytes=24 << 20),
            cost_estimate=pl.CostEstimate(
                flops=0, bytes_accessed=12 * parts * dl * units, transcendentals=0
            ),
        )(jnp.stack(index).astype(jnp.int32), wi, wd)

    w_peer = chip_swap(features(rep ^ 2, rep ^ 3))
    ra, rb, ga, gb = routes_a[0], routes_b[0], gates_a[0], gates_b[0]
    sel_a, sel_b, sel2_b, wt_a, wt_b = call(
        tables_kernel,
        [like((tok, slots)), like((tok, slots))] + [like((tok, 2 * slots))] * 3,
        [ra, rb, ga, gb],
        6 * tok * tok * slots * 2,
    )
    z_out = call(
        pick_kernel,
        [like((nz, 6 * CAP, dl))],
        [sel_a, sel_b, input_a[0], b_input[0], b_grad[0]],
        6 * tok * slots * dl,
    )[0]
    z_all = lax.all_to_all(z_out, "z", 0, 0, tiled=True)
    w_self = features(rep, rep ^ 1)
    z_all, w_peer, w_self = lax.optimization_barrier((z_all, w_peer, w_self))

    def one(kernel, shape, args, flops):
        return call(kernel, [shape], args, flops)[0]

    own = one(spread_kernel, like((NY, 3 * n, dl)), [z_all], NY * 3 * n * dl)
    own = lax.all_to_all(own, "yh", 0, 0, tiled=True)
    oth = core_swap(own)

    work = 2 * NY * n * 2 * dl * 2 * units
    peer_a = one(first_a_kernel, like((NY, n, 2 * units)), [own, oth, w_peer], work)
    peer_a = chip_swap(peer_a)
    peer_b = one(first_b_kernel, like((NY, n, 3 * units)), [own, oth, w_peer], work)
    peer_b = chip_swap(peer_b)
    self_a = one(first_a_kernel, like((NY, n, 2 * units), F32), [own, oth, w_self], work)
    self_b = one(first_b_kernel, like((NY, n, 3 * units), F32), [own, oth, w_self], work)

    rows = NY * n
    hid = one(
        middle_a_kernel,
        like((rows, units)),
        [self_a.reshape(rows, -1), peer_a.reshape(rows, -1)],
        work // 100,
    )
    hid_peer = chip_swap(hid)
    dgu = one(
        middle_b_kernel,
        like((rows, 3 * units)),
        [self_b.reshape(rows, -1), peer_b.reshape(rows, -1)],
        work // 100,
    )
    dgu_peer = chip_swap(dgu)
    args_a, args_b = [hid, hid_peer], [dgu, dgu_peer]
    w_own, w_oth = [w_self[:dl], w_peer[:dl]], [w_self[dl:], w_peer[dl:]]
    core_a = core_swap(one(last_a_kernel, like((rows, dl)), args_a + w_oth, work // 2))
    core_b = core_swap(one(last_b_kernel, like((rows, dl + units)), args_b + w_oth, work))
    kept_a = one(last_a_kernel, like((rows, dl), F32), args_a + w_own, work // 2)
    kept_b = one(last_b_kernel, like((rows, dl + units), F32), args_b + w_own, work)
    back = one(
        add_kernel, like((rows, 2 * dl + units)), [kept_a, core_a, kept_b, core_b], rows * dl
    )
    back = lax.all_to_all(back.reshape(sources, CAP, -1), ("z", "yh"), 0, 0, tiled=True)
    back = back.reshape(rows, -1)

    y, dx, dgate = call(
        combine_kernel,
        [like((tok, dl)), like((tok, dl)), like((tok, routes_b.shape[2]))],
        [back, wt_a, wt_b, sel2_b, rb],
        4 * tok * rows * dl,
    )
    return y[None], dx[None], dgate[None]


def solution(mesh):
    pipe, rep, ep = mesh.devices.shape
    split = Mesh(mesh.devices.reshape(pipe, rep, ep // NY, NY), ("pipe", "rep", "z", "yh"))
    rows = P("pipe", ("z", "yh"), "rep")
    small = P("pipe", ("z", "yh"), None)
    weights = P("pipe", ("z", "yh"), None, "rep", None)
    return jax.shard_map(
        on_device,
        mesh=split,
        in_specs=(rows, rows, rows, small, small, small, small, weights, weights),
        out_specs=(rows, rows, small),
        check_vma=False,
    )
```

```python
import jax
import jax.numpy as jnp
from jax import lax
from jax.experimental import pallas as pl
from jax.experimental.pallas import tpu as pltpu
from jax.sharding import Mesh
from jax.sharding import PartitionSpec as P

CAP = 8
NY = 4
PAD = 16
F32 = jnp.float32
BF16 = jnp.bfloat16
VMEM = pl.BlockSpec(memory_space=pltpu.VMEM)
SMEM = pl.BlockSpec(memory_space=pltpu.SMEM)
HBM = pl.BlockSpec(memory_space=pl.ANY)


def call(kernel, outs, args, flops, specs=None):
    moved = sum(x.size * x.dtype.itemsize for x in (*args, *outs))
    return pl.pallas_call(
        kernel,
        out_shape=outs,
        in_specs=specs or [VMEM] * len(args),
        out_specs=[VMEM] * len(outs),
        compiler_params=pltpu.CompilerParams(vmem_limit_bytes=24 << 20),
        cost_estimate=pl.CostEstimate(flops=flops, bytes_accessed=moved, transcendentals=0),
    )(*args)


def like(shape, dtype=BF16):
    return jax.ShapeDtypeStruct(shape, dtype)


def ring(axis, by):
    size = lax.axis_size(axis)
    return [(i, (i + by) % size) for i in range(size)]


def core_swap(value):
    return lax.ppermute(value, "rep", [(i, i ^ 1) for i in range(4)])


def chip_swap(value):
    return lax.ppermute(value, "rep", [(i, i ^ 2) for i in range(4)])


def diag_swap(value):
    return lax.ppermute(value, "rep", [(i, i ^ 3) for i in range(4)])


def mm(x, w):
    return jnp.dot(x, w, preferred_element_type=F32)


def mt(x, w):
    return lax.dot_general(x, w, (((1,), (1,)), ((), ())), preferred_element_type=F32)


def lanes_of(width):
    return lax.broadcasted_iota(jnp.int32, (1, width), 1)


def slot_table(routes, gates, width, per_expert):
    rows = routes.shape[0]
    lane = lanes_of(width)
    expert = (lane // per_expert).astype(F32)
    hit = jnp.zeros((rows, width), F32)
    weight = jnp.zeros((rows, width), F32)
    for k in range(routes.shape[1]):
        named = routes[:, k : k + 1] == expert
        hit = jnp.where(named, 1.0, hit)
        if gates is not None:
            weight = jnp.where(named, gates[:, k : k + 1], weight)
    row = lax.broadcasted_iota(jnp.int32, (rows, rows), 0)
    col = lax.broadcasted_iota(jnp.int32, (rows, rows), 1)
    lower = jnp.where(col < row, 1.0, 0.0).astype(BF16)
    before = mm(lower, hit.astype(BF16))
    select = jnp.where(before == (lane % CAP).astype(F32), hit, 0.0)
    return select, weight * select


def column(value):
    return value[...].astype(F32).T


def tables_kernel(ra, rb, sel_a, sel_b):
    for r, sel in ((ra, sel_a), (rb, sel_b)):
        sel[...] = slot_table(column(r), None, sel.shape[1], CAP)[0].astype(BF16)


def weights_kernel(ra, rb, ga, gb, sel_b, wt_a, wt_b):
    for r, g, sel, wt in ((ra, ga, None, wt_a), (rb, gb, sel_b, wt_b)):
        select, weight = slot_table(column(r), column(g), wt.shape[1], 2 * CAP)
        wt[...] = weight.astype(BF16)
        if sel is not None:
            sel[...] = select.astype(BF16)


def picked(sel, x):
    return lax.dot_general(sel[...], x[...], (((0,), (0,)), ((), ())), preferred_element_type=F32)


def pick_b_kernel(sel_b, b, g, rows_b, rows_g):
    rows_b[...] = picked(sel_b, b)
    rows_g[...] = picked(sel_b, g)


def pick_kernel(sel_a, a, rows_b, rows_g, out):
    parts = [picked(sel_a, a), rows_b[...], rows_g[...]]
    for z in range(out.shape[0]):
        rows = [
            p[(2 * z + m) * CAP : (2 * z + m + 1) * CAP] for m in range(2) for p in parts
        ]
        out[z] = jnp.concatenate(rows, axis=0).astype(BF16)


def features_kernel(index, wi, wd, out, sems):
    count, dl, _ = out.shape
    units = wd.shape[1]
    copies = []
    for i in range(count):
        rows = pl.ds(pl.multiple_of(index[i] * dl, dl), dl)
        to = out.at[i]
        copies.append(pltpu.make_async_copy(wi.at[rows], to.at[:, : 2 * units], sems.at[2 * i]))
        copies.append(pltpu.make_async_copy(wd.at[rows], to.at[:, 2 * units :], sems.at[2 * i + 1]))
    for copy in copies:
        copy.start()
    for copy in copies:
        copy.wait()


def gather_kernel(rep, mine, core, chip, diag, out):
    r = rep[0]
    for step, w in enumerate((mine, core, chip, diag)):
        out[r ^ step] = w[...]


def spread_kernel(z_rows, out):
    nz = z_rows.shape[0]
    wide = [z_rows[z].astype(F32) for z in range(nz)]
    for m in range(2):
        rows = [
            wide[z][(3 * m + q) * CAP : (3 * m + q + 1) * CAP] for q in range(3) for z in range(nz)
        ]
        both = jnp.concatenate(rows, axis=0).astype(BF16)
        out[2 * m] = both
        out[2 * m + 1] = both


def first_kernel(index, own, w, out):
    units = w.shape[2] // 3
    n = own.shape[1] // 3
    for i in range(2):
        at = 5 * units * i
        wi, wd = w[index[i], :, : 2 * units], w[index[i], :, 2 * units :]
        for s in range(NY):
            gu = mm(own[s, : 2 * n], wi).astype(out.dtype)
            rows = slice(s * n, (s + 1) * n)
            out[rows, at : at + 2 * units] = gu[:n]
            out[rows, at + 2 * units : at + 4 * units] = gu[n:]
            out[rows, at + 4 * units : at + 5 * units] = mm(own[s, 2 * n :], wd).astype(out.dtype)


def add_kernel(kept, core, out):
    wide = out.shape[1]
    out[...] = (kept[:, wide:] + core[:, wide:].astype(F32)).astype(BF16)


def by_source(value):
    nz = value.shape[0] // (NY * CAP)
    rows = [
        value[(s * nz + z) * CAP : (s * nz + z + 1) * CAP] for z in range(nz) for s in range(NY)
    ]
    return jnp.concatenate(rows, axis=0)


def middle_kernel(kept, core, chip, out):
    wide = chip.shape[1]
    units = out.shape[1] // 3
    rows = kept.shape[0]
    v = kept[:, :wide] + core[:, :wide].astype(F32) + chip[...].astype(F32)
    ag, au, g, u, dh = [v[:, i * units : (i + 1) * units] for i in range(5)]
    hid_a = ag * jax.nn.sigmoid(ag) * au
    sq = jax.nn.sigmoid(g)
    hid = (g * sq * u).astype(BF16).astype(F32)
    dgate = jnp.broadcast_to(jnp.sum(hid * dh, axis=1, keepdims=True), g.shape)
    d_gate = dh * u * sq * (1.0 + g * (1.0 - sq))
    d_up = dh * g * sq
    out[:rows] = by_source(jnp.concatenate([hid_a, d_gate, d_up], axis=1)).astype(BF16)
    last = by_source(dgate).T[:PAD]
    fill = jnp.zeros((PAD, out.shape[1] - rows), F32)
    out[rows:] = jnp.concatenate([last, fill], axis=1).astype(BF16)


def last_kernel(hidden, w, out):
    blocks, dl, units = w.shape[0], w.shape[1], w.shape[2] // 3
    rows = out.shape[0]
    o = jnp.zeros((rows, dl), F32)
    dx = jnp.zeros((rows, dl), F32)
    dg = jnp.zeros((1, rows), F32)
    for j in range(blocks):
        o = o + mt(hidden[j, :rows, :units], w[j, :, 2 * units :])
        dx = dx + mt(hidden[j, :rows, units:], w[j, :, : 2 * units])
        dg = dg + hidden[j, rows:, :rows].astype(F32)[:1]
    out[:, :dl] = o.astype(BF16)
    out[:, dl : 2 * dl] = dx.astype(BF16)
    out[:, 2 * dl :] = jnp.broadcast_to(dg, (units, rows)).T.astype(BF16)


def combine_kernel(back, wt_a, wt_b, sel2_b, routes, y, dx, dgate):
    dl = y.shape[1]
    y[...] = mm(wt_a[...], back[:, :dl]).astype(BF16)
    dx[...] = mm(wt_b[...], back[:, dl : 2 * dl]).astype(BF16)
    dg = back[:, 2 * dl :]
    expert = (lanes_of(sel2_b.shape[1]) // (2 * CAP)).astype(F32)
    routes = column(routes)
    sel = sel2_b[...].astype(F32)
    topk = dgate.shape[0]
    out = jnp.zeros((sel.shape[0], dg.shape[1]), F32)
    lane = lanes_of(dg.shape[1])
    for k in range(topk):
        chosen = jnp.where(routes[:, k : k + 1] == expert, sel, 0.0).astype(BF16)
        out = jnp.where(lane == k, mm(chosen, dg), out)
    dgate[...] = out.T[:topk].astype(BF16)


def on_device(a_sent, b_input, b_grad, routes_a, routes_b, gates_a, gates_b, w_in, w_down):
    nz = lax.axis_size("z")
    sources, experts = nz * NY, nz * 2
    slots = experts * CAP
    rep = lax.axis_index("rep")
    tok, dl = a_sent.shape[1:]
    wi, wd = w_in[0, 0, :, 0, :], w_down[0, 0, :, 0, :]
    units = wd.shape[1]
    n = nz * CAP

    input_a = lax.ppermute(a_sent, "pipe", ring("pipe", 1))

    def features(*index):
        count = len(index)
        return pl.pallas_call(
            features_kernel,
            out_shape=like((count, dl, 3 * units)),
            in_specs=[SMEM, HBM, HBM],
            out_specs=HBM,
            scratch_shapes=[pltpu.SemaphoreType.DMA((2 * count,))],
            compiler_params=pltpu.CompilerParams(vmem_limit_bytes=24 << 20),
            cost_estimate=pl.CostEstimate(
                flops=0, bytes_accessed=12 * count * dl * units, transcendentals=0
            ),
        )(jnp.stack(index).astype(jnp.int32), wi, wd)

    def one(kernel, shape, args, flops, scalars=None):
        if scalars is None:
            return call(kernel, [shape], args, flops)[0]
        args = [jnp.stack(scalars).astype(jnp.int32), *args]
        return call(kernel, [shape], args, flops, [SMEM] + [VMEM] * (len(args) - 1))[0]

    w_chip = chip_swap(features(rep ^ 2, rep ^ 3))
    ra, rb, ga, gb = routes_a[0].T, routes_b[0].T, gates_a[0].T, gates_b[0].T
    sel_a, sel_b = call(
        tables_kernel, [like((tok, slots))] * 2, [ra, rb], 4 * tok * tok * slots
    )
    rows_b, rows_g = call(
        pick_b_kernel,
        [like((slots, dl), F32)] * 2,
        [sel_b, b_input[0], b_grad[0]],
        4 * tok * slots * dl,
    )
    z_out = one(
        pick_kernel,
        like((nz, 6 * CAP, dl)),
        [sel_a, input_a[0], rows_b, rows_g],
        2 * tok * slots * dl,
    )
    z_all = lax.all_to_all(z_out, "z", 0, 0, tiled=True)
    z_all, w_chip = lax.optimization_barrier((z_all, w_chip))
    w_here = features(rep, rep ^ 1)
    w_core = core_swap(w_here[1])
    w_diag = core_swap(w_chip[1])
    w_all = one(
        gather_kernel,
        like((4, dl, 3 * units)),
        [w_here[0], w_core, w_chip[0], w_diag],
        4 * dl * units,
        [rep],
    )

    own = one(spread_kernel, like((NY, 3 * n, dl)), [z_all], NY * 3 * n * dl)
    own = lax.all_to_all(own, "yh", 0, 0, tiled=True)

    rows, wide = NY * n, 5 * units
    work = 2 * rows * dl * 2 * wide
    core = one(first_kernel, like((rows, 2 * wide)), [own, w_all], work, [rep ^ 1, rep ^ 3])
    core = core_swap(core)
    kept = one(first_kernel, like((rows, 2 * wide), F32), [own, w_all], work, [rep, rep ^ 2])
    chip = chip_swap(one(add_kernel, like((rows, wide)), [kept, core], rows * wide))
    mine = one(middle_kernel, like((rows + PAD, 3 * units)), [kept, core, chip], rows * units * 40)
    hidden = lax.all_gather(mine, "rep")
    back = one(
        last_kernel, like((rows, 2 * dl + units)), [hidden, w_all], 2 * rows * dl * 12 * units
    )
    back, ra, rb, ga, gb = lax.optimization_barrier((back, ra, rb, ga, gb))
    back = lax.all_to_all(back.reshape(sources, CAP, -1), ("z", "yh"), 0, 0, tiled=True)
    back = back.reshape(rows, -1)

    sel_b, wt_a, wt_b = call(
        weights_kernel, [like((tok, 2 * slots))] * 3, [ra, rb, ga, gb], 8 * tok * tok * slots
    )
    y, dx, dgate = call(
        combine_kernel,
        [like((tok, dl)), like((tok, dl)), like((routes_b.shape[2], tok))],
        [back, wt_a, wt_b, sel_b, rb],
        4 * tok * rows * dl,
    )
    return y[None], dx[None], dgate.T[None]


def solution(mesh):
    pipe, rep, ep = mesh.devices.shape
    split = Mesh(mesh.devices.reshape(pipe, rep, ep // NY, NY), ("pipe", "rep", "z", "yh"))
    rows = P("pipe", ("z", "yh"), "rep")
    small = P("pipe", ("z", "yh"), None)
    weights = P("pipe", ("z", "yh"), None, "rep", None)
    return jax.shard_map(
        on_device,
        mesh=split,
        in_specs=(rows, rows, rows, small, small, small, small, weights, weights),
        out_specs=(rows, rows, small),
        check_vma=False,
    )
```

```python
import jax
import jax.numpy as jnp
from jax import lax
from jax.experimental import pallas as pl
from jax.experimental.pallas import tpu as pltpu
from jax.sharding import Mesh
from jax.sharding import PartitionSpec as P

CAP = 8
NY = 4
PAD = 16
F32 = jnp.float32
BF16 = jnp.bfloat16
VMEM = pl.BlockSpec(memory_space=pltpu.VMEM)
SMEM = pl.BlockSpec(memory_space=pltpu.SMEM)
HBM = pl.BlockSpec(memory_space=pl.ANY)


def call(kernel, outs, args, flops, specs=None):
    moved = sum(x.size * x.dtype.itemsize for x in (*args, *outs))
    return pl.pallas_call(
        kernel,
        out_shape=outs,
        in_specs=specs or [VMEM] * len(args),
        out_specs=[VMEM] * len(outs),
        compiler_params=pltpu.CompilerParams(vmem_limit_bytes=24 << 20),
        cost_estimate=pl.CostEstimate(flops=flops, bytes_accessed=moved, transcendentals=0),
    )(*args)


def like(shape, dtype=BF16):
    return jax.ShapeDtypeStruct(shape, dtype)


def ring(axis, by):
    size = lax.axis_size(axis)
    return [(i, (i + by) % size) for i in range(size)]


def core_swap(value):
    return lax.ppermute(value, "rep", [(i, i ^ 1) for i in range(4)])


def chip_swap(value):
    return lax.ppermute(value, "rep", [(i, i ^ 2) for i in range(4)])


def diag_swap(value):
    return lax.ppermute(value, "rep", [(i, i ^ 3) for i in range(4)])


def mm(x, w):
    return jnp.dot(x, w, preferred_element_type=F32)


def mt(x, w):
    return lax.dot_general(x, w, (((1,), (1,)), ((), ())), preferred_element_type=F32)


def lanes_of(width):
    return lax.broadcasted_iota(jnp.int32, (1, width), 1)


def slot_table(routes, gates, width, per_expert):
    rows = routes.shape[0]
    lane = lanes_of(width)
    expert = (lane // per_expert).astype(F32)
    hit = jnp.zeros((rows, width), F32)
    weight = jnp.zeros((rows, width), F32)
    for k in range(routes.shape[1]):
        named = routes[:, k : k + 1] == expert
        hit = jnp.where(named, 1.0, hit)
        if gates is not None:
            weight = jnp.where(named, gates[:, k : k + 1], weight)
    row = lax.broadcasted_iota(jnp.int32, (rows, rows), 0)
    col = lax.broadcasted_iota(jnp.int32, (rows, rows), 1)
    lower = jnp.where(col < row, 1.0, 0.0).astype(BF16)
    before = mm(lower, hit.astype(BF16))
    select = jnp.where(before == (lane % CAP).astype(F32), hit, 0.0)
    return select, weight * select


def column(value):
    return value[...].astype(F32).T


def tables_kernel(ra, rb, sel_a, sel_b):
    for r, sel in ((ra, sel_a), (rb, sel_b)):
        sel[...] = slot_table(column(r), None, sel.shape[1], CAP)[0].astype(BF16)


def weights_kernel(ra, rb, ga, gb, sel_b, wt_a, wt_b):
    for r, g, sel, wt in ((ra, ga, None, wt_a), (rb, gb, sel_b, wt_b)):
        select, weight = slot_table(column(r), column(g), wt.shape[1], 2 * CAP)
        wt[...] = weight.astype(BF16)
        if sel is not None:
            sel[...] = select.astype(BF16)


def picked(sel, x):
    return lax.dot_general(sel[...], x[...], (((0,), (0,)), ((), ())), preferred_element_type=F32)


def pick_b_kernel(sel_b, b, g, rows_b, rows_g):
    rows_b[...] = picked(sel_b, b)
    rows_g[...] = picked(sel_b, g)


def pick_kernel(sel_a, a, rows_b, rows_g, out):
    parts = [picked(sel_a, a), rows_b[...], rows_g[...]]
    for z in range(out.shape[0]):
        rows = [
            p[(2 * z + m) * CAP : (2 * z + m + 1) * CAP] for m in range(2) for p in parts
        ]
        out[z] = jnp.concatenate(rows, axis=0).astype(BF16)


def features_kernel(index, wi, wd, out, sems):
    count, dl, _ = out.shape
    units = wd.shape[1]
    copies = []
    for i in range(count):
        rows = pl.ds(pl.multiple_of(index[i] * dl, dl), dl)
        to = out.at[i]
        copies.append(pltpu.make_async_copy(wi.at[rows], to.at[:, : 2 * units], sems.at[2 * i]))
        copies.append(pltpu.make_async_copy(wd.at[rows], to.at[:, 2 * units :], sems.at[2 * i + 1]))
    for copy in copies:
        copy.start()
    for copy in copies:
        copy.wait()


def gather_kernel(rep, mine, core, chip, diag, out):
    r = rep[0]
    for step, w in enumerate((mine, core, chip, diag)):
        out[r ^ step] = w[...]


def spread_kernel(z_rows, out):
    nz = z_rows.shape[0]
    wide = [z_rows[z].astype(F32) for z in range(nz)]
    for m in range(2):
        rows = [
            wide[z][(3 * m + q) * CAP : (3 * m + q + 1) * CAP] for q in range(3) for z in range(nz)
        ]
        both = jnp.concatenate(rows, axis=0).astype(BF16)
        out[2 * m] = both
        out[2 * m + 1] = both


def first_kernel(index, own, w, out):
    units = w.shape[2] // 3
    n = own.shape[1] // 3
    for i in range(out.shape[1] // (5 * units)):
        at = 5 * units * i
        wi, wd = w[index[i], :, : 2 * units], w[index[i], :, 2 * units :]
        for s in range(NY):
            gu = mm(own[s, : 2 * n], wi).astype(out.dtype)
            rows = slice(s * n, (s + 1) * n)
            out[rows, at : at + 2 * units] = gu[:n]
            out[rows, at + 2 * units : at + 4 * units] = gu[n:]
            out[rows, at + 4 * units : at + 5 * units] = mm(own[s, 2 * n :], wd).astype(out.dtype)


def add_kernel(kept, core, out):
    out[...] = (kept[...] + core[:, out.shape[1] :].astype(F32)).astype(BF16)


def by_source(value):
    nz = value.shape[0] // (NY * CAP)
    rows = [
        value[(s * nz + z) * CAP : (s * nz + z + 1) * CAP] for z in range(nz) for s in range(NY)
    ]
    return jnp.concatenate(rows, axis=0)


def middle_kernel(kept, core, chip, out):
    wide = chip.shape[1]
    units = out.shape[1] // 3
    rows = kept.shape[0]
    v = kept[...] + core[:, :wide].astype(F32) + chip[...].astype(F32)
    ag, au, g, u, dh = [v[:, i * units : (i + 1) * units] for i in range(5)]
    hid_a = ag * jax.nn.sigmoid(ag) * au
    sq = jax.nn.sigmoid(g)
    hid = (g * sq * u).astype(BF16).astype(F32)
    dgate = jnp.broadcast_to(jnp.sum(hid * dh, axis=1, keepdims=True), g.shape)
    d_gate = dh * u * sq * (1.0 + g * (1.0 - sq))
    d_up = dh * g * sq
    out[:rows] = by_source(jnp.concatenate([hid_a, d_gate, d_up], axis=1)).astype(BF16)
    last = by_source(dgate).T[:PAD]
    fill = jnp.zeros((PAD, out.shape[1] - rows), F32)
    out[rows:] = jnp.concatenate([last, fill], axis=1).astype(BF16)


def last_kernel(hidden, w, out):
    blocks, dl, units = w.shape[0], w.shape[1], w.shape[2] // 3
    rows = out.shape[0]
    o = jnp.zeros((rows, dl), F32)
    dx = jnp.zeros((rows, dl), F32)
    dg = jnp.zeros((1, rows), F32)
    for j in range(blocks):
        o = o + mt(hidden[j, :rows, :units], w[j, :, 2 * units :])
        dx = dx + mt(hidden[j, :rows, units:], w[j, :, : 2 * units])
        dg = dg + hidden[j, rows:, :rows].astype(F32)[:1]
    out[:, :dl] = o.astype(BF16)
    out[:, dl : 2 * dl] = dx.astype(BF16)
    out[:, 2 * dl :] = jnp.broadcast_to(dg, (units, rows)).T.astype(BF16)


def combine_kernel(back, wt_a, wt_b, sel2_b, routes, y, dx, dgate):
    dl = y.shape[1]
    y[...] = mm(wt_a[...], back[:, :dl]).astype(BF16)
    dx[...] = mm(wt_b[...], back[:, dl : 2 * dl]).astype(BF16)
    dg = back[:, 2 * dl :]
    expert = (lanes_of(sel2_b.shape[1]) // (2 * CAP)).astype(F32)
    routes = column(routes)
    sel = sel2_b[...].astype(F32)
    topk = dgate.shape[0]
    out = jnp.zeros((sel.shape[0], dg.shape[1]), F32)
    lane = lanes_of(dg.shape[1])
    for k in range(topk):
        chosen = jnp.where(routes[:, k : k + 1] == expert, sel, 0.0).astype(BF16)
        out = jnp.where(lane == k, mm(chosen, dg), out)
    dgate[...] = out.T[:topk].astype(BF16)


def on_device(a_sent, b_input, b_grad, routes_a, routes_b, gates_a, gates_b, w_in, w_down):
    nz = lax.axis_size("z")
    sources, experts = nz * NY, nz * 2
    slots = experts * CAP
    rep = lax.axis_index("rep")
    tok, dl = a_sent.shape[1:]
    wi, wd = w_in[0, 0, :, 0, :], w_down[0, 0, :, 0, :]
    units = wd.shape[1]
    n = nz * CAP

    input_a = lax.ppermute(a_sent, "pipe", ring("pipe", 1))

    def features(*index):
        count = len(index)
        return pl.pallas_call(
            features_kernel,
            out_shape=like((count, dl, 3 * units)),
            in_specs=[SMEM, HBM, HBM],
            out_specs=HBM,
            scratch_shapes=[pltpu.SemaphoreType.DMA((2 * count,))],
            compiler_params=pltpu.CompilerParams(vmem_limit_bytes=24 << 20),
            cost_estimate=pl.CostEstimate(
                flops=0, bytes_accessed=12 * count * dl * units, transcendentals=0
            ),
        )(jnp.stack(index).astype(jnp.int32), wi, wd)

    def one(kernel, shape, args, flops, scalars=None):
        if scalars is None:
            return call(kernel, [shape], args, flops)[0]
        args = [jnp.stack(scalars).astype(jnp.int32), *args]
        return call(kernel, [shape], args, flops, [SMEM] + [VMEM] * (len(args) - 1))[0]

    w_chip = chip_swap(features(rep ^ 2, rep ^ 3))
    ra, rb, ga, gb = routes_a[0].T, routes_b[0].T, gates_a[0].T, gates_b[0].T
    sel_a, sel_b = call(
        tables_kernel, [like((tok, slots))] * 2, [ra, rb], 4 * tok * tok * slots
    )
    rows_b, rows_g = call(
        pick_b_kernel,
        [like((slots, dl), F32)] * 2,
        [sel_b, b_input[0], b_grad[0]],
        4 * tok * slots * dl,
    )
    z_out = one(
        pick_kernel,
        like((nz, 6 * CAP, dl)),
        [sel_a, input_a[0], rows_b, rows_g],
        2 * tok * slots * dl,
    )
    z_all = lax.all_to_all(z_out, "z", 0, 0, tiled=True)
    z_all, w_chip, ra, rb, ga, gb = lax.optimization_barrier((z_all, w_chip, ra, rb, ga, gb))
    sel_b, wt_a, wt_b = call(
        weights_kernel, [like((tok, 2 * slots))] * 3, [ra, rb, ga, gb], 8 * tok * tok * slots
    )
    w_here = features(rep, rep ^ 1)
    w_core = core_swap(w_here[1])
    w_diag = core_swap(w_chip[1])
    w_all = one(
        gather_kernel,
        like((4, dl, 3 * units)),
        [w_here[0], w_core, w_chip[0], w_diag],
        4 * dl * units,
        [rep],
    )

    own = one(spread_kernel, like((NY, 3 * n, dl)), [z_all], NY * 3 * n * dl)
    own = lax.all_to_all(own, "yh", 0, 0, tiled=True)
    own, sel_b, wt_a, wt_b = lax.optimization_barrier((own, sel_b, wt_a, wt_b))

    rows, wide = NY * n, 5 * units
    work = 2 * rows * dl * 2 * wide
    core = one(first_kernel, like((rows, 2 * wide)), [own, w_all], work, [rep ^ 1, rep ^ 3])
    core = core_swap(core)
    kept = one(first_kernel, like((rows, wide), F32), [own, w_all], work // 2, [rep ^ 2])
    to_chip = one(add_kernel, like((rows, wide)), [kept, core], rows * wide)
    chip = chip_swap(to_chip)
    own, to_chip = lax.optimization_barrier((own, to_chip))
    kept = one(first_kernel, like((rows, wide), F32), [own, w_all], work // 2, [rep])
    mine = one(middle_kernel, like((rows + PAD, 3 * units)), [kept, core, chip], rows * units * 40)
    hidden = lax.all_gather(mine, "rep")
    back = one(
        last_kernel, like((rows, 2 * dl + units)), [hidden, w_all], 2 * rows * dl * 12 * units
    )
    back = lax.all_to_all(back.reshape(sources, CAP, -1), ("z", "yh"), 0, 0, tiled=True)
    back = back.reshape(rows, -1)

    y, dx, dgate = call(
        combine_kernel,
        [like((tok, dl)), like((tok, dl)), like((routes_b.shape[2], tok))],
        [back, wt_a, wt_b, sel_b, rb],
        4 * tok * rows * dl,
    )
    return y[None], dx[None], dgate.T[None]


def solution(mesh):
    pipe, rep, ep = mesh.devices.shape
    split = Mesh(mesh.devices.reshape(pipe, rep, ep // NY, NY), ("pipe", "rep", "z", "yh"))
    rows = P("pipe", ("z", "yh"), "rep")
    small = P("pipe", ("z", "yh"), None)
    weights = P("pipe", ("z", "yh"), None, "rep", None)
    return jax.shard_map(
        on_device,
        mesh=split,
        in_specs=(rows, rows, rows, small, small, small, small, weights, weights),
        out_specs=(rows, rows, small),
        check_vma=False,
    )
```

```python
import jax
import jax.numpy as jnp
from jax import lax
from jax.experimental import pallas as pl
from jax.experimental.pallas import tpu as pltpu
from jax.sharding import Mesh
from jax.sharding import PartitionSpec as P

CAP = 8
NY = 4
PAD = 16
F32 = jnp.float32
BF16 = jnp.bfloat16
VMEM = pl.BlockSpec(memory_space=pltpu.VMEM)
SMEM = pl.BlockSpec(memory_space=pltpu.SMEM)
HBM = pl.BlockSpec(memory_space=pl.ANY)


def call(kernel, outs, args, flops, specs=None):
    moved = sum(x.size * x.dtype.itemsize for x in (*args, *outs))
    return pl.pallas_call(
        kernel,
        out_shape=outs,
        in_specs=specs or [VMEM] * len(args),
        out_specs=[VMEM] * len(outs),
        compiler_params=pltpu.CompilerParams(vmem_limit_bytes=24 << 20),
        cost_estimate=pl.CostEstimate(flops=flops, bytes_accessed=moved, transcendentals=0),
    )(*args)


def like(shape, dtype=BF16):
    return jax.ShapeDtypeStruct(shape, dtype)


def ring(axis, by):
    size = lax.axis_size(axis)
    return [(i, (i + by) % size) for i in range(size)]


def core_swap(value):
    return lax.ppermute(value, "rep", [(i, i ^ 1) for i in range(4)])


def chip_swap(value):
    return lax.ppermute(value, "rep", [(i, i ^ 2) for i in range(4)])


def diag_swap(value):
    return lax.ppermute(value, "rep", [(i, i ^ 3) for i in range(4)])


def mm(x, w):
    return jnp.dot(x, w, preferred_element_type=F32)


def mt(x, w):
    return lax.dot_general(x, w, (((1,), (1,)), ((), ())), preferred_element_type=F32)


def lanes_of(width):
    return lax.broadcasted_iota(jnp.int32, (1, width), 1)


def slot_table(routes, gates, width, per_expert):
    rows = routes.shape[0]
    lane = lanes_of(width)
    expert = (lane // per_expert).astype(F32)
    hit = jnp.zeros((rows, width), F32)
    weight = jnp.zeros((rows, width), F32)
    for k in range(routes.shape[1]):
        named = routes[:, k : k + 1] == expert
        hit = jnp.where(named, 1.0, hit)
        if gates is not None:
            weight = jnp.where(named, gates[:, k : k + 1], weight)
    row = lax.broadcasted_iota(jnp.int32, (rows, rows), 0)
    col = lax.broadcasted_iota(jnp.int32, (rows, rows), 1)
    lower = jnp.where(col < row, 1.0, 0.0).astype(BF16)
    before = mm(lower, hit.astype(BF16))
    select = jnp.where(before == (lane % CAP).astype(F32), hit, 0.0)
    return select, weight * select


def column(value):
    return value[...].astype(F32).T


def tables_kernel(ra, rb, sel_a, sel_b):
    for r, sel in ((ra, sel_a), (rb, sel_b)):
        sel[...] = slot_table(column(r), None, sel.shape[1], CAP)[0].astype(BF16)


def weights_kernel(ra, rb, ga, gb, sel_b, wt_a, wt_b):
    for r, g, sel, wt in ((ra, ga, None, wt_a), (rb, gb, sel_b, wt_b)):
        select, weight = slot_table(column(r), column(g), wt.shape[1], 2 * CAP)
        wt[...] = weight.astype(BF16)
        if sel is not None:
            sel[...] = select.astype(BF16)


def picked(sel, x):
    return lax.dot_general(sel[...], x[...], (((0,), (0,)), ((), ())), preferred_element_type=F32)


def pick_b_kernel(sel_b, b, g, rows_b, rows_g):
    rows_b[...] = picked(sel_b, b)
    rows_g[...] = picked(sel_b, g)


def pick_kernel(sel_a, a, rows_b, rows_g, out):
    parts = [picked(sel_a, a), rows_b[...], rows_g[...]]
    for z in range(out.shape[0]):
        rows = [
            p[(2 * z + m) * CAP : (2 * z + m + 1) * CAP] for m in range(2) for p in parts
        ]
        out[z] = jnp.concatenate(rows, axis=0).astype(BF16)


def features_kernel(index, wi, wd, out, sems):
    count, dl, _ = out.shape
    units = wd.shape[1]
    copies = []
    for i in range(count):
        rows = pl.ds(pl.multiple_of(index[i] * dl, dl), dl)
        to = out.at[i]
        copies.append(pltpu.make_async_copy(wi.at[rows], to.at[:, : 2 * units], sems.at[2 * i]))
        copies.append(pltpu.make_async_copy(wd.at[rows], to.at[:, 2 * units :], sems.at[2 * i + 1]))
    for copy in copies:
        copy.start()
    for copy in copies:
        copy.wait()


def gather_kernel(rep, mine, core, chip, diag, out):
    r = rep[0]
    for step, w in enumerate((mine, core, chip, diag)):
        out[r ^ step] = w[...]


def spread_kernel(z_rows, out):
    nz = z_rows.shape[0]
    wide = [z_rows[z].astype(F32) for z in range(nz)]
    for m in range(2):
        rows = [
            wide[z][(3 * m + q) * CAP : (3 * m + q + 1) * CAP] for q in range(3) for z in range(nz)
        ]
        both = jnp.concatenate(rows, axis=0).astype(BF16)
        out[2 * m] = both
        out[2 * m + 1] = both


def first_kernel(index, own, w, out):
    units = w.shape[2] // 3
    n = own.shape[1] // 3
    for i in range(out.shape[1] // (5 * units)):
        at = 5 * units * i
        wi, wd = w[index[i], :, : 2 * units], w[index[i], :, 2 * units :]
        for s in range(NY):
            gu = mm(own[s, : 2 * n], wi).astype(out.dtype)
            rows = slice(s * n, (s + 1) * n)
            out[rows, at : at + 2 * units] = gu[:n]
            out[rows, at + 2 * units : at + 4 * units] = gu[n:]
            out[rows, at + 4 * units : at + 5 * units] = mm(own[s, 2 * n :], wd).astype(out.dtype)


def add_kernel(kept, core, out):
    out[...] = (kept[...] + core[...].astype(F32)).astype(BF16)


def by_source(value):
    nz = value.shape[0] // (NY * CAP)
    rows = [
        value[(s * nz + z) * CAP : (s * nz + z + 1) * CAP] for z in range(nz) for s in range(NY)
    ]
    return jnp.concatenate(rows, axis=0)


def middle_kernel(kept, core, chip, out):
    wide = chip.shape[1]
    units = out.shape[1] // 3
    rows = kept.shape[0]
    v = kept[...] + core[:, :wide].astype(F32) + chip[...].astype(F32)
    ag, au, g, u, dh = [v[:, i * units : (i + 1) * units] for i in range(5)]
    hid_a = ag * jax.nn.sigmoid(ag) * au
    sq = jax.nn.sigmoid(g)
    hid = (g * sq * u).astype(BF16).astype(F32)
    dgate = jnp.broadcast_to(jnp.sum(hid * dh, axis=1, keepdims=True), g.shape)
    d_gate = dh * u * sq * (1.0 + g * (1.0 - sq))
    d_up = dh * g * sq
    out[:rows] = by_source(jnp.concatenate([hid_a, d_gate, d_up], axis=1)).astype(BF16)
    last = by_source(dgate).T[:PAD]
    fill = jnp.zeros((PAD, out.shape[1] - rows), F32)
    out[rows:] = jnp.concatenate([last, fill], axis=1).astype(BF16)


def last_kernel(hidden, w, out):
    blocks, dl, units = w.shape[0], w.shape[1], w.shape[2] // 3
    rows = out.shape[0]
    o = jnp.zeros((rows, dl), F32)
    dx = jnp.zeros((rows, dl), F32)
    dg = jnp.zeros((1, rows), F32)
    for j in range(blocks):
        o = o + mt(hidden[j, :rows, :units], w[j, :, 2 * units :])
        dx = dx + mt(hidden[j, :rows, units:], w[j, :, : 2 * units])
        dg = dg + hidden[j, rows:, :rows].astype(F32)[:1]
    out[:, :dl] = o.astype(BF16)
    out[:, dl : 2 * dl] = dx.astype(BF16)
    out[:, 2 * dl :] = jnp.broadcast_to(dg, (units, rows)).T.astype(BF16)


def combine_kernel(back, wt_a, wt_b, sel2_b, routes, y, dx, dgate):
    dl = y.shape[1]
    y[...] = mm(wt_a[...], back[:, :dl]).astype(BF16)
    dx[...] = mm(wt_b[...], back[:, dl : 2 * dl]).astype(BF16)
    dg = back[:, 2 * dl :]
    expert = (lanes_of(sel2_b.shape[1]) // (2 * CAP)).astype(F32)
    routes = column(routes)
    sel = sel2_b[...].astype(F32)
    topk = dgate.shape[0]
    out = jnp.zeros((sel.shape[0], dg.shape[1]), F32)
    lane = lanes_of(dg.shape[1])
    for k in range(topk):
        chosen = jnp.where(routes[:, k : k + 1] == expert, sel, 0.0).astype(BF16)
        out = jnp.where(lane == k, mm(chosen, dg), out)
    dgate[...] = out.T[:topk].astype(BF16)


def on_device(a_sent, b_input, b_grad, routes_a, routes_b, gates_a, gates_b, w_in, w_down):
    nz = lax.axis_size("z")
    sources, experts = nz * NY, nz * 2
    slots = experts * CAP
    rep = lax.axis_index("rep")
    tok, dl = a_sent.shape[1:]
    wi, wd = w_in[0, 0, :, 0, :], w_down[0, 0, :, 0, :]
    units = wd.shape[1]
    n = nz * CAP

    input_a = lax.ppermute(a_sent, "pipe", ring("pipe", 1))

    def features(*index):
        count = len(index)
        return pl.pallas_call(
            features_kernel,
            out_shape=like((count, dl, 3 * units)),
            in_specs=[SMEM, HBM, HBM],
            out_specs=HBM,
            scratch_shapes=[pltpu.SemaphoreType.DMA((2 * count,))],
            compiler_params=pltpu.CompilerParams(vmem_limit_bytes=24 << 20),
            cost_estimate=pl.CostEstimate(
                flops=0, bytes_accessed=12 * count * dl * units, transcendentals=0
            ),
        )(jnp.stack(index).astype(jnp.int32), wi, wd)

    def one(kernel, shape, args, flops, scalars=None):
        if scalars is None:
            return call(kernel, [shape], args, flops)[0]
        args = [jnp.stack(scalars).astype(jnp.int32), *args]
        return call(kernel, [shape], args, flops, [SMEM] + [VMEM] * (len(args) - 1))[0]

    w_chip = chip_swap(features(rep ^ 2, rep ^ 3))
    ra, rb, ga, gb = routes_a[0].T, routes_b[0].T, gates_a[0].T, gates_b[0].T
    sel_a, sel_b = call(
        tables_kernel, [like((tok, slots))] * 2, [ra, rb], 4 * tok * tok * slots
    )
    rows_b, rows_g = call(
        pick_b_kernel,
        [like((slots, dl), F32)] * 2,
        [sel_b, b_input[0], b_grad[0]],
        4 * tok * slots * dl,
    )
    z_out = one(
        pick_kernel,
        like((nz, 6 * CAP, dl)),
        [sel_a, input_a[0], rows_b, rows_g],
        2 * tok * slots * dl,
    )
    z_all = lax.all_to_all(z_out, "z", 0, 0, tiled=True)
    z_all, w_chip, ra, rb, ga, gb = lax.optimization_barrier((z_all, w_chip, ra, rb, ga, gb))
    sel_b, wt_a, wt_b = call(
        weights_kernel, [like((tok, 2 * slots))] * 3, [ra, rb, ga, gb], 8 * tok * tok * slots
    )
    w_here = features(rep, rep ^ 1)
    w_core = core_swap(w_here[1])
    w_diag = core_swap(w_chip[1])
    w_all = one(
        gather_kernel,
        like((4, dl, 3 * units)),
        [w_here[0], w_core, w_chip[0], w_diag],
        4 * dl * units,
        [rep],
    )

    own = one(spread_kernel, like((NY, 3 * n, dl)), [z_all], NY * 3 * n * dl)
    own = lax.all_to_all(own, "yh", 0, 0, tiled=True)
    own, sel_b, wt_a, wt_b = lax.optimization_barrier((own, sel_b, wt_a, wt_b))

    rows, wide = NY * n, 5 * units
    work = 2 * rows * dl * 2 * wide
    half = like((rows, wide))
    core = core_swap(one(first_kernel, half, [own, w_all], work // 2, [rep ^ 3]))
    kept = one(first_kernel, like((rows, wide), F32), [own, w_all], work // 2, [rep ^ 2])
    to_chip = one(add_kernel, half, [kept, core], rows * wide)
    chip = chip_swap(to_chip)
    own, to_chip = lax.optimization_barrier((own, to_chip))
    core = core_swap(one(first_kernel, half, [own, w_all], work // 2, [rep ^ 1]))
    kept = one(first_kernel, like((rows, wide), F32), [own, w_all], work // 2, [rep])
    mine = one(middle_kernel, like((rows + PAD, 3 * units)), [kept, core, chip], rows * units * 40)
    hidden = lax.all_gather(mine, "rep")
    back = one(
        last_kernel, like((rows, 2 * dl + units)), [hidden, w_all], 2 * rows * dl * 12 * units
    )
    back = lax.all_to_all(back.reshape(sources, CAP, -1), ("z", "yh"), 0, 0, tiled=True)
    back = back.reshape(rows, -1)

    y, dx, dgate = call(
        combine_kernel,
        [like((tok, dl)), like((tok, dl)), like((routes_b.shape[2], tok))],
        [back, wt_a, wt_b, sel_b, rb],
        4 * tok * rows * dl,
    )
    return y[None], dx[None], dgate.T[None]


def solution(mesh):
    pipe, rep, ep = mesh.devices.shape
    split = Mesh(mesh.devices.reshape(pipe, rep, ep // NY, NY), ("pipe", "rep", "z", "yh"))
    rows = P("pipe", ("z", "yh"), "rep")
    small = P("pipe", ("z", "yh"), None)
    weights = P("pipe", ("z", "yh"), None, "rep", None)
    return jax.shard_map(
        on_device,
        mesh=split,
        in_specs=(rows, rows, rows, small, small, small, small, weights, weights),
        out_specs=(rows, rows, small),
        check_vma=False,
    )
```
